32 devices in a mesh: lat: 4 (over y, x), lon: 8 (over z, core).
Axes of the slice: x: 2, y: 2, z: 4, core: 2. Of those that a mesh axis runs over, the one named last changes fastest.
Arguments:
- states: bfloat16 [2, 144, 384, 192], P(None, 'lat', 'lon'), may hold values from -6 to 6
- cotangent: bfloat16 [2, 144, 384, 192], P(None, 'lat', 'lon'), may hold values from -9 to 9
- land_mask: int32 [144, 384], P('lat', 'lon'), may hold values 0 or 1
- pole_mask: int32 [144], P('lat'), may hold values from 0 to 1, as said below
- bias_table: float32 [12, 11, 3456], P('lat'), may hold values from -4 to 410
- norm_gain: float32 [192], replicated, may hold values from 0.5 to 1.5
- norm_shift: float32 [192], replicated, may hold values from -3 to 3
- in_weight: bfloat16 [192, 576], replicated, may hold values from -0.4375 to 0.4375
- in_bias: float32 [576], replicated, may hold values from -3 to 3
- out_weight: bfloat16 [192, 192], replicated, may hold values from -0.4375 to 0.4375
- land_gain: float32 [6], replicated, may hold values from -2 to 2
Outputs:
- grad_states: bfloat16 [2, 144, 384, 192], P(None, 'lat', 'lon')
- grad_in_weight: float32 [192, 576], replicated
- grad_in_bias: float32 [576], replicated
- grad_out_weight: float32 [192, 192], replicated
- grad_out_bias: float32 [192], replicated
- grad_norm_gain: float32 [192], replicated
- grad_norm_shift: float32 [192], replicated
- grad_land_gain: float32 [6], replicated
- grad_bias_table: float32 [12, 11, 3456], P('lat')
The draws below stay inside these ranges and needn't reach their ends.
Inputs may be any that keep to these rules, and one draw needn't show every extreme that they name: `pole_mask`: pole padding: zero on the last P rows of the grid and one on all others, for some P from 1 to 5.
All inputs are finite; a program needn't handle non-finite values. No bound on the sum of `land_mask` on one device may be relied on, other than what follows from the above.
Results may differ from the reference program's by a relative error of at most 0.0095.
Values may be sent and summed in bfloat16 or wider, within the bound.
A program may use at most 128 MiB of HBM per device.

```python
import jax
import jax.numpy as jnp
from jax import lax

C = 192
HEADS = 6
PL = 2
WLAT = 12
WLON = 6
S_LAT = 6
S_LON = 3
WT = 144
DL = 11
NPOS = 3456
NLAT = 144
NLON = 384
NLATW = 12


def draw_cotangent(key, part):
    key = jax.random.fold_in(key, 11)
    row_frac = jnp.arange(NLAT, dtype=jnp.float32) / NLAT
    growth = (0.5 + row_frac)[None, :, None, None]
    values = jnp.clip(jax.random.normal(key, (PL, NLAT, NLON, C), jnp.float32), -6.0, 6.0) * growth
    return values.astype(jnp.bfloat16)


def draw_pole_mask(key, part):
    key = jax.random.fold_in(key, 12)
    padded = jax.random.randint(key, (), 1, 6, dtype=jnp.int32)
    return (jnp.arange(NLAT, dtype=jnp.int32) < NLAT - padded).astype(jnp.int32)


def draw_bias_table(key, part):
    key = jax.random.fold_in(key, 13)
    table_shape = (NLATW, DL, NPOS)
    values = jnp.clip(jax.random.normal(key, table_shape, jnp.float32), -4.0, 4.0)
    return values


def touch_ends(values, own_key, smallest, largest):
    place = [jax.random.randint(jax.random.fold_in(own_key, axis), (), 0, length) for axis, length in enumerate(values.shape)]
    main_axis = values.shape.index(max(values.shape))
    next_to = place[:main_axis] + [(place[main_axis] + 1) % values.shape[main_axis]] + place[main_axis + 1:]
    return values.at[tuple(place)].set(smallest).at[tuple(next_to)].set(largest)


def levels(key, dims, pieces, smallest, top_value):
    def one(axis_at, shards_of):
        steps = jax.random.uniform(jax.random.fold_in(jax.random.fold_in(key, 6), axis_at), (shards_of,), jnp.float32, smallest / len(pieces), top_value / len(pieces))
        return jnp.repeat(jnp.exp(steps), dims[axis_at] // shards_of).reshape((-1,) + (1,) * (len(dims) - axis_at - 1))

    level = one(*pieces[0])
    for cut in pieces[1:]:
        level = level * one(*cut)
    return level


def centred(own_key, shape, scale, limit, cuts=(), kind=jnp.bfloat16):
    drawn = jax.random.normal(own_key, shape, jnp.float32) * scale
    if len(cuts) > 0:
        drawn = levels(own_key, shape, cuts, -0.22, 0.18) * drawn
    return jnp.clip(drawn, min=-limit, max=limit).astype(kind)


def setup_inputs(seed: int = 0) -> dict:
    arg_keys = jax.random.split(jax.random.key(seed), 12)
    states = centred(arg_keys[0], (PL, NLAT, NLON, C), 1.0, 6.0, ((1, 4), (2, 8)))
    cotangent = draw_cotangent(jax.random.fold_in(arg_keys[11], 71), 0)
    land_mask = touch_ends((jax.random.randint(arg_keys[2], (NLAT, NLON), 0, 10) < 3).astype(jnp.int32), jax.random.fold_in(arg_keys[2], 1), 0, 1)
    pole_mask = draw_pole_mask(jax.random.fold_in(arg_keys[11], 71), 0)
    bias_table = draw_bias_table(jax.random.fold_in(arg_keys[11], 71), 0)
    norm_gain = jnp.clip(1.0 + 0.1 * jax.random.normal(arg_keys[5], (C,), jnp.float32), 0.5, 1.5)
    norm_shift = centred(arg_keys[6], (C,), 0.5, 3.0, (), jnp.float32)
    in_weight = centred(arg_keys[7], (C, 3 * C), C ** -0.5, 0.4375)
    in_bias = centred(arg_keys[8], (3 * C,), 0.5, 3.0, (), jnp.float32)
    out_weight = centred(arg_keys[9], (C, C), C ** -0.5, 0.4375)
    land_gain = jnp.clip(jax.random.uniform(arg_keys[10], (HEADS,), jnp.float32, -2.0, 2.0), -2.0, 2.0)
    return {"states": states, "cotangent": cotangent, "land_mask": land_mask, "pole_mask": pole_mask, "bias_table": bias_table, "norm_gain": norm_gain, "norm_shift": norm_shift, "in_weight": in_weight, "in_bias": in_bias, "out_weight": out_weight, "land_gain": land_gain}


EPSILON = 1e-05
TARGET_RMS = 0.5
RMS_EPSILON = 1e-06

def lon_onehot():
    offsets = jnp.arange(DL, dtype=jnp.int32)[:, None, None]
    query_col = jnp.arange(WLON, dtype=jnp.int32)[None, :, None]
    key_col = jnp.arange(WLON, dtype=jnp.int32)[None, None, :]
    return (query_col - key_col + WLON - 1 == offsets).astype(jnp.float32)

def expand_bias(table_row):
    shaped = table_row.reshape(DL, HEADS, PL, PL, WLAT, WLAT)
    full_bias = jnp.einsum('dhabij,dxy->haixbjy', shaped, lon_onehot(), precision=lax.Precision.HIGHEST)
    return full_bias.reshape(HEADS, WT, WT)

def collapse_bias(grad_full):
    shaped = grad_full.reshape(HEADS, PL, WLAT, WLON, PL, WLAT, WLON)
    folded = jnp.einsum('haixbjy,dxy->dhabij', shaped, lon_onehot(), precision=lax.Precision.HIGHEST)
    return folded.reshape(DL, NPOS)

def allowed_pairs(row_part, row_valid):
    part_tok = jnp.tile(jnp.repeat(row_part, WLON), PL)
    valid_tok = jnp.tile(jnp.repeat(row_valid, WLON), PL)
    return (part_tok[:, None] == part_tok[None, :]) & (valid_tok[None, :] > 0)

def to_windows(grid):
    col_count = grid.shape[2]
    feat_count = grid.shape[3]
    split = grid.reshape(PL, WLAT, col_count // WLON, WLON, feat_count)
    return split.transpose(2, 0, 1, 3, 4).reshape(col_count // WLON, WT, feat_count)

def from_windows(windows, col_count):
    feat_count = windows.shape[2]
    split = windows.reshape(col_count // WLON, PL, WLAT, WLON, feat_count)
    return split.transpose(1, 2, 0, 3, 4).reshape(PL, WLAT, col_count, feat_count)

def window_block(tokens, cot_win, land_tok, allowed, table_row, norm_gain, norm_shift, in_weight, in_bias, out_weight, land_gain):
    f32 = jnp.float32
    win_count = tokens.shape[0]
    head_dim = C // HEADS
    qk_scale = head_dim ** (-0.5)
    floats = tokens.astype(f32)
    center = floats - lax.optimization_barrier(jnp.mean(floats, axis=-1, keepdims=True))
    inv_std = lax.rsqrt(lax.optimization_barrier(jnp.mean(center * center, axis=-1, keepdims=True)) + EPSILON)
    normed = center * inv_std
    hidden = (normed * norm_gain + norm_shift).astype(jnp.bfloat16)
    flat_hidden = hidden.reshape(win_count * WT, C)
    projected = jnp.dot(flat_hidden, in_weight, preferred_element_type=f32) + in_bias
    packed = projected.astype(jnp.bfloat16).reshape(win_count, WT, 3, HEADS, head_dim)
    queries = packed[:, :, 0]
    key_rows = packed[:, :, 1]
    value_rows = packed[:, :, 2]
    scores = jnp.einsum('wqhd,wkhd->whqk', queries.astype(f32), key_rows.astype(f32)) * qk_scale
    scores = scores + expand_bias(table_row)[None] + land_gain[None, :, None, None] * land_tok[:, None, None, :]
    pair_gate = allowed[None, None]
    row_top = lax.optimization_barrier(jnp.max(jnp.where(pair_gate, scores, -jnp.inf), axis=-1, keepdims=True))
    exp_terms = jnp.where(pair_gate, jnp.exp(scores - row_top), 0.0)
    probs = exp_terms / lax.optimization_barrier(jnp.sum(exp_terms, axis=-1, keepdims=True))
    probs_low = probs.astype(jnp.bfloat16)
    mixed_out = jnp.einsum('whqk,wkhd->wqhd', probs_low.astype(f32), value_rows.astype(f32))
    mixed_low = mixed_out.reshape(win_count * WT, C).astype(jnp.bfloat16)
    flat_cot = cot_win.reshape(win_count * WT, C)
    grad_out_weight = jnp.dot(mixed_low.T, flat_cot, preferred_element_type=f32)
    grad_out_bias = lax.optimization_barrier(jnp.sum(flat_cot.astype(f32), axis=0))
    grad_mixed = jnp.dot(flat_cot, out_weight.T, preferred_element_type=f32).astype(jnp.bfloat16)
    grad_mixed = grad_mixed.reshape(win_count, WT, HEADS, head_dim)
    grad_probs = jnp.einsum('wqhd,wkhd->whqk', grad_mixed.astype(f32), value_rows.astype(f32))
    grad_values = jnp.einsum('whqk,wqhd->wkhd', probs_low.astype(f32), grad_mixed.astype(f32))
    grad_scores = probs * (grad_probs - lax.optimization_barrier(jnp.sum(grad_probs * probs, axis=-1, keepdims=True)))
    grad_land = jnp.einsum('whqk,wk->h', grad_scores, land_tok, precision=lax.Precision.HIGHEST)
    grad_table = collapse_bias(lax.optimization_barrier(jnp.sum(grad_scores, axis=0)))
    scores_low = grad_scores.astype(jnp.bfloat16)
    grad_queries = jnp.einsum('whqk,wkhd->wqhd', scores_low.astype(f32), key_rows.astype(f32)) * qk_scale
    grad_keys = jnp.einsum('whqk,wqhd->wkhd', scores_low.astype(f32), queries.astype(f32)) * qk_scale
    grad_packed = jnp.stack([grad_queries, grad_keys, grad_values], axis=2).reshape(win_count * WT, 3 * C)
    grad_in_bias = lax.optimization_barrier(jnp.sum(grad_packed, axis=0))
    packed_low = grad_packed.astype(jnp.bfloat16)
    grad_in_weight = jnp.dot(flat_hidden.T, packed_low, preferred_element_type=f32)
    grad_hidden = jnp.dot(packed_low, in_weight.T, preferred_element_type=f32).reshape(win_count, WT, C)
    grad_gain = lax.optimization_barrier(jnp.sum(grad_hidden * normed, axis=(0, 1)))
    grad_shift = lax.optimization_barrier(jnp.sum(grad_hidden, axis=(0, 1)))
    scaled = grad_hidden * norm_gain
    grad_tokens = inv_std * (scaled - lax.optimization_barrier(jnp.mean(scaled, axis=-1, keepdims=True)) - normed * lax.optimization_barrier(jnp.mean(scaled * normed, axis=-1, keepdims=True)))
    dense_terms = (grad_in_weight, grad_in_bias, grad_out_weight, grad_out_bias, grad_gain, grad_shift, grad_land)
    return (grad_tokens.astype(jnp.bfloat16), dense_terms, grad_table)

def normalize_rms(gradient):
    rms_value = jnp.sqrt(jnp.mean(gradient * gradient) + RMS_EPSILON)
    return gradient * (TARGET_RMS / rms_value)

def reference(states, cotangent, land_mask, pole_mask, bias_table, norm_gain, norm_shift, in_weight, in_bias, out_weight, land_gain):
    rolled = jnp.roll(states, (-S_LAT, -S_LON), axis=(1, 2))
    rolled_cot = jnp.roll(cotangent, (-S_LAT, -S_LON), axis=(1, 2))
    rolled_land = jnp.roll(land_mask, (-S_LAT, -S_LON), axis=(0, 1)).astype(jnp.float32)
    rolled_pole = jnp.roll(pole_mask, -S_LAT)
    row_ids = jnp.arange(NLAT, dtype=jnp.int32)
    row_part = (row_ids >= NLAT - S_LAT).astype(jnp.int32)

    def one_row(band_index):
        start = (band_index * WLAT).astype(jnp.int32)
        tokens = to_windows(lax.dynamic_slice_in_dim(rolled, start, WLAT, 1))
        cot_win = to_windows(lax.dynamic_slice_in_dim(rolled_cot, start, WLAT, 1))
        land_rows = lax.dynamic_slice_in_dim(rolled_land, start, WLAT, 0)
        land_tok = to_windows(jnp.broadcast_to(land_rows[None, :, :, None], (PL, WLAT, NLON, 1)))[:, :, 0]
        pairs = allowed_pairs(lax.dynamic_slice_in_dim(row_part, start, WLAT, 0), lax.dynamic_slice_in_dim(rolled_pole, start, WLAT, 0))
        table_row = lax.dynamic_index_in_dim(bias_table, band_index, 0, keepdims=False)
        grad_tok, dense_terms, grad_table = window_block(tokens, cot_win, land_tok, pairs, table_row, norm_gain, norm_shift, in_weight, in_bias, out_weight, land_gain)
        return (from_windows(grad_tok, NLON), dense_terms, grad_table)
    grad_rows, dense_rows, table_rows = lax.map(one_row, jnp.arange(NLATW, dtype=jnp.int32))
    attn_grad = grad_rows.transpose(1, 0, 2, 3, 4).reshape(PL, NLAT, NLON, C)
    attn_back = jnp.roll(attn_grad, (S_LAT, S_LON), axis=(1, 2))
    grad_states = (cotangent.astype(jnp.float32) + attn_back.astype(jnp.float32)).astype(jnp.bfloat16)
    dense_sums = [lax.optimization_barrier(jnp.sum(grad_part, axis=0)) for grad_part in dense_rows]
    return (grad_states, normalize_rms(dense_sums[0]), normalize_rms(dense_sums[1]), normalize_rms(dense_sums[2]), normalize_rms(dense_sums[3]), normalize_rms(dense_sums[4]), normalize_rms(dense_sums[5]), normalize_rms(dense_sums[6]), normalize_rms(table_rows))
```

```python
import jax
import jax.numpy as jnp
from jax import lax
from jax.experimental import pallas as pl
from jax.experimental.pallas import tpu as pltpu
from jax.sharding import PartitionSpec as P

C = 192
HEADS = 6
HD = C // HEADS
PL = 2
WLAT = 12
WLON = 6
S_LAT = 6
S_LON = 3
WT = 144
DL = 11
NPOS = 3456
COL = PL * WLAT
HL = HEADS * WT
TL = DL * COL

EPSILON = 1e-05
TARGET_RMS = 0.5
RMS_EPSILON = 1e-06
FAR = -1e30
F32 = jnp.float32
BF16 = jnp.bfloat16


def moved(array, axes, sizes, by):
    if isinstance(axes, str):
        size = sizes[axes]
        return lax.ppermute(array, axes, [(i, (i + by) % size) for i in range(size)])
    lat, lon = sizes["lat"], sizes["lon"]
    pairs = [
        (a * lon + b, ((a + by) % lat) * lon + (b + by) % lon)
        for a in range(lat)
        for b in range(lon)
    ]
    return lax.ppermute(array, axes, pairs)


def dot(a, b):
    return jnp.dot(a, b, preferred_element_type=F32)


def dot_nt(a, b):
    return lax.dot_general(a, b, (((1,), (1,)), ((), ())), preferred_element_type=F32)


def by_head(rows, head_masks):
    return jnp.concatenate([rows * m for m in head_masks], axis=0)


def diagonal(full):
    return jnp.concatenate(
        [full[HD * h : HD * (h + 1), WT * h : WT * (h + 1)] for h in range(HEADS)], axis=0
    )


def kernel(
    windows,
    per_step,
    tok_ref,
    cot_ref,
    land_ref,
    table_ref,
    gain_ref,
    shift_ref,
    win_ref,
    win_t_ref,
    bin_ref,
    wout_t_ref,
    lg_ref,
    grad_ref,
    dwin_ref,
    dbin_ref,
    dwout_ref,
    dbout_ref,
    dgain_ref,
    dshift_ref,
    dland_ref,
    dtable_ref,
    bias_s,
    acc_s,
):
    band = pl.program_id(0)
    step = pl.program_id(1)
    scale = HD ** (-0.5)

    @pl.when((band == 0) & (step == 0))
    def _():
        for ref in (dwin_ref, dbin_ref, dwout_ref, dbout_ref, dgain_ref, dshift_ref, dland_ref):
            ref[...] = jnp.zeros_like(ref)

    @pl.when(step == 0)
    def _():
        acc_s[...] = jnp.zeros_like(acc_s)
        for h in range(HEADS):
            for j in range(WLON):
                start = h * TL + (WLON - 1 - j) * COL
                bias_s[j * COL : (j + 1) * COL, h * WT : (h + 1) * WT] = table_ref[
                    0, :, start : start + WT
                ]

    lane = lax.broadcasted_iota(jnp.int32, (1, C), 1) // HD
    head_masks = [(lane == h).astype(F32).astype(BF16) for h in range(HEADS)]
    land_lane = lax.broadcasted_iota(jnp.int32, (1, windows), 1)

    for k in range(per_step):
        tok = tok_ref[k].astype(F32)
        center = tok - jnp.mean(tok, axis=-1, keepdims=True)
        inv_std = lax.rsqrt(jnp.mean(center * center, axis=-1, keepdims=True) + EPSILON)
        normed = center * inv_std
        hidden_f = normed * gain_ref[...] + shift_ref[...]
        hidden = hidden_f.astype(BF16)
        packed = (dot(hidden, win_ref[...]) + bin_ref[...]).astype(BF16)
        queries = packed[:, :C]
        keys = packed[:, C : 2 * C]
        values = packed[:, 2 * C :]
        q_heads = by_head(queries, head_masks)
        land = jnp.sum(
            jnp.where(land_lane == step * per_step + k, land_ref[0], 0.0), axis=1, keepdims=True
        )
        scores = dot_nt(keys, q_heads) * scale + bias_s[...] + land * lg_ref[...]
        top = jnp.max(scores, axis=0, keepdims=True)
        expd = jnp.exp(scores - top)
        probs = expd * (1.0 / jnp.sum(expd, axis=0, keepdims=True))
        probs_low = probs.astype(BF16)
        mixed_t = diagonal(dot(values.astype(F32).T.astype(BF16), probs_low)).astype(BF16)
        cot = cot_ref[k]
        dwout_ref[...] += dot(mixed_t, cot)
        dbout_ref[...] += jnp.sum(cot.astype(F32), axis=0, keepdims=True)
        grad_mixed = dot(cot, wout_t_ref[...]).astype(BF16)
        m_heads = by_head(grad_mixed, head_masks)
        grad_probs = dot_nt(values, m_heads)
        grad_values = dot(probs_low, m_heads)
        inner = jnp.sum(grad_probs * probs, axis=0, keepdims=True)
        grad_scores = probs * (grad_probs - inner)
        acc_s[...] += grad_scores
        dland_ref[...] += jnp.sum(grad_scores * land, axis=0, keepdims=True)
        scores_low = grad_scores.astype(BF16)
        grad_q = diagonal(dot(keys.astype(F32).T.astype(BF16), scores_low)).T * scale
        grad_k = dot(scores_low, q_heads) * scale
        grad_packed = jnp.concatenate([grad_q, grad_k, grad_values], axis=1)
        dbin_ref[...] += jnp.sum(grad_packed, axis=0, keepdims=True)
        packed_low = grad_packed.astype(BF16)
        dwin_ref[...] += dot(hidden_f.T.astype(BF16), packed_low)
        grad_hidden = dot(packed_low, win_t_ref[...])
        dgain_ref[...] += jnp.sum(grad_hidden * normed, axis=0, keepdims=True)
        dshift_ref[...] += jnp.sum(grad_hidden, axis=0, keepdims=True)
        scaled = grad_hidden * gain_ref[...]
        grad_tok = inv_std * (
            scaled
            - jnp.mean(scaled, axis=-1, keepdims=True)
            - normed * jnp.mean(scaled * normed, axis=-1, keepdims=True)
        )
        grad_ref[k] = grad_tok.astype(BF16)

    @pl.when(step == pl.num_programs(1) - 1)
    def _():
        dtable_ref[...] = jnp.zeros_like(dtable_ref)
        for h in range(HEADS):
            for j in range(WLON):
                start = h * TL + (WLON - 1 - j) * COL
                dtable_ref[0, :, start : start + WT] += acc_s[
                    j * COL : (j + 1) * COL, h * WT : (h + 1) * WT
                ]


def attend(tokens, cots, land, table, gain, shift, w_in, b_in, w_out, land_gain, bands):
    count = tokens.shape[0]
    windows = count // bands
    per_step = 2 if windows % 2 == 0 else 1
    steps = windows // per_step

    def fixed(shape):
        return pl.BlockSpec(shape, lambda a, w: (0,) * len(shape))

    def per_band(shape):
        return pl.BlockSpec(shape, lambda a, w: (a,) + (0,) * (len(shape) - 1))

    win_spec = pl.BlockSpec((per_step, WT, C), lambda a, w: (a * steps + w, 0, 0))
    shapes = [(C, 3 * C), (1, 3 * C), (C, C), (1, C), (1, C), (1, C), (1, HL)]

    def body(*refs):
        kernel(windows, per_step, *refs)

    return pl.pallas_call(
        body,
        grid=(bands, steps),
        in_specs=[
            win_spec,
            win_spec,
            per_band((1, WT, windows)),
            per_band((1, COL, HEADS * TL)),
            fixed((1, C)),
            fixed((1, C)),
            fixed((C, 3 * C)),
            fixed((3 * C, C)),
            fixed((1, 3 * C)),
            fixed((C, C)),
            fixed((1, HL)),
        ],
        out_specs=[win_spec]
        + [fixed(s) for s in shapes]
        + [per_band((1, COL, HEADS * TL))],
        out_shape=[jax.ShapeDtypeStruct(tokens.shape, BF16)]
        + [jax.ShapeDtypeStruct(s, F32) for s in shapes]
        + [jax.ShapeDtypeStruct((bands, COL, HEADS * TL), F32)],
        scratch_shapes=[pltpu.VMEM((WT, HL), F32), pltpu.VMEM((WT, HL), F32)],
        compiler_params=pltpu.CompilerParams(
            dimension_semantics=("arbitrary", "arbitrary"), vmem_limit_bytes=48 * 1024 * 1024
        ),
    )(
        tokens,
        cots,
        land,
        table,
        gain.reshape(1, C),
        shift.reshape(1, C),
        w_in,
        w_in.T,
        b_in.reshape(1, 3 * C),
        w_out.T,
        jnp.repeat(land_gain, WT).reshape(1, HL),
    )


def normalize_rms(gradient):
    rms_value = jnp.sqrt(jnp.mean(gradient * gradient) + RMS_EPSILON)
    return gradient * (TARGET_RMS / rms_value)


def local(
    sizes,
    states,
    cotangent,
    land_mask,
    pole_mask,
    bias_table,
    norm_gain,
    norm_shift,
    in_weight,
    in_bias,
    out_weight,
    land_gain,
):
    rows = states.shape[1]
    cols = states.shape[2]
    bands = rows // WLAT
    windows = cols // WLON
    both = ("lat", "lon")
    lon_piece = jnp.stack([states[:, :, :S_LON], cotangent[:, :, :S_LON]])
    lat_piece = jnp.stack([states[:, :S_LAT, S_LON:], cotangent[:, :S_LAT, S_LON:]])
    land_low = land_mask.astype(BF16)
    pole_low = pole_mask.astype(BF16)
    lon_rim = moved(lon_piece, "lon", sizes, -1)
    lat_rim = moved(lat_piece, "lat", sizes, -1)
    corner = moved(lon_piece[:, :, :S_LAT], both, sizes, -1)
    land_ahead = jnp.concatenate([land_low[:, S_LON:], moved(land_low[:, :S_LON], "lon", sizes, -1)], axis=1)
    small = jnp.concatenate([land_ahead[:S_LAT], pole_low[:S_LAT, None]], axis=1)
    small_rim = moved(small, "lat", sizes, -1)
    rolled_land = jnp.concatenate([land_ahead[S_LAT:], small_rim[:, :cols]], axis=0).astype(F32)
    rolled_pole = jnp.concatenate([pole_low[S_LAT:], small_rim[:, cols]], axis=0).astype(F32)

    def windowed(own, at):
        top = jnp.concatenate([own[:, S_LAT:, S_LON:], lon_rim[at][:, S_LAT:]], axis=2)
        low = jnp.concatenate([lat_rim[at], corner[at]], axis=2)
        grid = jnp.concatenate([top, low], axis=1)
        return (
            grid.reshape(PL, bands, WLAT, cols, C)
            .transpose(1, 3, 0, 2, 4)
            .reshape(bands * windows, WT, C)
        )

    land_win = rolled_land.reshape(bands, WLAT, windows, WLON).transpose(0, 3, 1, 2)
    land_win = jnp.broadcast_to(
        land_win[:, :, None], (bands, WLON, PL, WLAT, windows)
    ).reshape(bands, WT, windows)
    total_rows = rows * sizes["lat"]
    row_ids = lax.axis_index("lat") * rows + jnp.arange(rows, dtype=jnp.int32)
    part = (row_ids >= total_rows - S_LAT).reshape(bands, WLAT)
    valid = (rolled_pole > 0.5).reshape(bands, WLAT)
    allowed = (part[:, :, None] == part[:, None, :]) & valid[:, :, None]
    table = bias_table.reshape(bands, DL, HEADS, PL, PL, WLAT, WLAT).transpose(0, 4, 6, 2, 1, 3, 5)
    table = jnp.where(allowed[:, None, :, None, None, None, :], table, FAR)
    table = table.reshape(bands, COL, HEADS * TL)
    outs = attend(
        windowed(states, 0),
        windowed(cotangent, 1),
        land_win,
        table,
        norm_gain,
        norm_shift,
        in_weight,
        in_bias,
        out_weight,
        land_gain,
        bands,
    )
    grad_win, dwin, dbin, dwout, dbout, dgain, dshift, dland, dtable = outs
    grad = (
        grad_win.reshape(bands, cols, PL, WLAT, C).transpose(2, 0, 3, 1, 4).reshape(PL, rows, cols, C)
    )
    below = moved(grad[:, rows - S_LAT :, : cols - S_LON], "lat", sizes, 1)
    behind = moved(grad[:, : rows - S_LAT, cols - S_LON :], "lon", sizes, 1)
    back_corner = moved(grad[:, rows - S_LAT :, cols - S_LON :], both, sizes, 1)
    upper = jnp.concatenate([back_corner, below], axis=2)
    lower = jnp.concatenate([behind, grad[:, : rows - S_LAT, : cols - S_LON]], axis=2)
    back = jnp.concatenate([upper, lower], axis=1)
    grad_states = (cotangent.astype(F32) + back.astype(F32)).astype(BF16)
    dland = jnp.sum(dland.reshape(HEADS, WT), axis=1)
    sums = lax.psum((dwin, dbin, dwout, dbout, dgain, dshift, dland), both)
    table_sum = lax.psum(dtable, "lon")
    table_sq = lax.psum(jnp.sum(table_sum * table_sum), "lat")
    table_count = bands * sizes["lat"] * DL * NPOS
    table_rms = jnp.sqrt(table_sq / table_count + RMS_EPSILON)
    table_out = table_sum * (TARGET_RMS / table_rms)
    table_out = table_out.reshape(bands, PL, WLAT, HEADS, DL, PL, WLAT).transpose(0, 4, 3, 5, 1, 6, 2)
    return (
        grad_states,
        normalize_rms(sums[0]),
        normalize_rms(sums[1].reshape(3 * C)),
        normalize_rms(sums[2]),
        normalize_rms(sums[3].reshape(C)),
        normalize_rms(sums[4].reshape(C)),
        normalize_rms(sums[5].reshape(C)),
        normalize_rms(sums[6]),
        table_out.reshape(bands, DL, NPOS),
    )


def solution(mesh):
    sizes = dict(mesh.shape)

    def run(*args):
        return local(sizes, *args)

    return jax.shard_map(
        run,
        mesh=mesh,
        in_specs=(
            P(None, "lat", "lon", None),
            P(None, "lat", "lon", None),
            P("lat", "lon"),
            P("lat"),
            P("lat", None, None),
            P(),
            P(),
            P(),
            P(),
            P(),
            P(),
        ),
        out_specs=(
            P(None, "lat", "lon", None),
            P(),
            P(),
            P(),
            P(),
            P(),
            P(),
            P(),
            P("lat", None, None),
        ),
        check_vma=False,
    )
```

```python
import functools

import jax
import jax.numpy as jnp
from jax import lax
from jax.experimental import pallas as pl
from jax.experimental.pallas import tpu as pltpu
from jax.sharding import PartitionSpec as P

C = 192
HEADS = 6
HD = C // HEADS
PL = 2
WLAT = 12
WLON = 6
S_LAT = 6
S_LON = 3
WT = 144
DL = 11
NPOS = 3456
COL = PL * WLAT
HL = HEADS * WT
TL = DL * COL
TW = -(-HEADS * TL // 128)
HB = NPOS // HEADS
SMALL = 24

EPSILON = 1e-05
TARGET_RMS = 0.5
RMS_EPSILON = 1e-06
FAR = -1e30
F32 = jnp.float32
BF16 = jnp.bfloat16


def moved(array, axes, sizes, by):
    if isinstance(axes, str):
        size = sizes[axes]
        return lax.ppermute(array, axes, [(i, (i + by) % size) for i in range(size)])
    lat, lon = sizes["lat"], sizes["lon"]
    pairs = [
        (a * lon + b, ((a + by) % lat) * lon + (b + by) % lon)
        for a in range(lat)
        for b in range(lon)
    ]
    return lax.ppermute(array, axes, pairs)


def dot(a, b):
    return jnp.dot(a, b, preferred_element_type=F32)


def dot_nt(a, b):
    return lax.dot_general(a, b, (((1,), (1,)), ((), ())), preferred_element_type=F32)


def by_head(rows, head_masks):
    return jnp.concatenate([rows * m for m in head_masks], axis=0)


def diagonal(full):
    return jnp.concatenate(
        [full[HD * h : HD * (h + 1), WT * h : WT * (h + 1)] for h in range(HEADS)], axis=0
    )


def table_masks():
    row = lax.broadcasted_iota(jnp.int32, (COL, HB), 0)
    place = lax.broadcasted_iota(jnp.int32, (COL, HB), 1)
    q_level = place // (HB // 2)
    k_level = place // WT % 2
    q_row = place // WLAT % WLAT
    k_row = place % WLAT
    keep = (row == q_level * WLAT + q_row).astype(F32)
    pick = (row == k_level * WLAT + k_row).astype(F32)
    return keep, pick


def kernel(
    windows,
    per_step,
    tok_ref,
    cot_ref,
    land_ref,
    table_ref,
    gain_ref,
    shift_ref,
    win_ref,
    win_t_ref,
    bin_ref,
    wout_t_ref,
    lg_ref,
    gate_ref,
    grad_ref,
    dense_ref,
    small_ref,
    dtable_ref,
    dwin_ref,
    dbin_ref,
    dwout_ref,
    dbout_ref,
    dgain_ref,
    dshift_ref,
    dland_ref,
    bias_s,
    acc_s,
    fold_s,
):
    band = pl.program_id(0)
    step = pl.program_id(1)
    scale = HD ** (-0.5)

    @pl.when((band == 0) & (step == 0))
    def _():
        for ref in (dwin_ref, dbin_ref, dwout_ref, dbout_ref, dgain_ref, dshift_ref, dland_ref):
            ref[...] = jnp.zeros_like(ref)

    @pl.when(step == 0)
    def _():
        acc_s[...] = jnp.zeros_like(acc_s)
        keep, pick = table_masks()
        for h in range(HEADS):
            own = table_ref[0, :, h * HB : (h + 1) * HB]
            spread = (own[:, None, :] * keep[None]).reshape(TL, HB)
            fold_s[:, h * TL : (h + 1) * TL] = (
                lax.dot_general(
                    pick,
                    spread,
                    (((1,), (1,)), ((), ())),
                    precision=lax.Precision.HIGHEST,
                    preferred_element_type=F32,
                )
                + gate_ref[0]
            )
        for h in range(HEADS):
            for j in range(WLON):
                start = h * TL + (WLON - 1 - j) * COL
                bias_s[j * COL : (j + 1) * COL, h * WT : (h + 1) * WT] = fold_s[
                    :, start : start + WT
                ]

    lane = lax.broadcasted_iota(jnp.int32, (1, C), 1) // HD
    head_masks = [(lane == h).astype(F32).astype(BF16) for h in range(HEADS)]
    land_lane = lax.broadcasted_iota(jnp.int32, (1, windows), 1)

    for k in range(per_step):
        tok = tok_ref[k].astype(F32)
        center = tok - jnp.mean(tok, axis=-1, keepdims=True)
        inv_std = lax.rsqrt(jnp.mean(center * center, axis=-1, keepdims=True) + EPSILON)
        normed = center * inv_std
        hidden_f = normed * gain_ref[...] + shift_ref[...]
        hidden = hidden_f.astype(BF16)
        packed = (dot(hidden, win_ref[...]) + bin_ref[...]).astype(BF16)
        queries = packed[:, :C]
        keys = packed[:, C : 2 * C]
        values = packed[:, 2 * C :]
        q_heads = by_head(queries, head_masks)
        land = jnp.sum(
            jnp.where(land_lane == step * per_step + k, land_ref[0], 0.0), axis=1, keepdims=True
        )
        scores = dot_nt(keys, q_heads) * scale + bias_s[...] + land * lg_ref[...]
        top = jnp.max(scores, axis=0, keepdims=True)
        expd = jnp.exp(scores - top)
        probs = expd * (1.0 / jnp.sum(expd, axis=0, keepdims=True))
        probs_low = probs.astype(BF16)
        mixed_t = diagonal(dot(values.astype(F32).T.astype(BF16), probs_low)).astype(BF16)
        cot = cot_ref[k]
        dwout_ref[...] += dot(mixed_t, cot)
        dbout_ref[...] += jnp.sum(cot.astype(F32), axis=0, keepdims=True)
        grad_mixed = dot(cot, wout_t_ref[...]).astype(BF16)
        m_heads = by_head(grad_mixed, head_masks)
        grad_probs = dot_nt(values, m_heads)
        grad_values = dot(probs_low, m_heads)
        inner = jnp.sum(grad_probs * probs, axis=0, keepdims=True)
        grad_scores = probs * (grad_probs - inner)
        acc_s[...] += grad_scores
        dland_ref[...] += jnp.sum(grad_scores * land, axis=0, keepdims=True)
        scores_low = grad_scores.astype(BF16)
        grad_q = diagonal(dot(keys.astype(F32).T.astype(BF16), scores_low)).T * scale
        grad_k = dot(scores_low, q_heads) * scale
        grad_packed = jnp.concatenate([grad_q, grad_k, grad_values], axis=1)
        dbin_ref[...] += jnp.sum(grad_packed, axis=0, keepdims=True)
        packed_low = grad_packed.astype(BF16)
        dwin_ref[...] += dot(hidden_f.T.astype(BF16), packed_low)
        grad_hidden = dot(packed_low, win_t_ref[...])
        dgain_ref[...] += jnp.sum(grad_hidden * normed, axis=0, keepdims=True)
        dshift_ref[...] += jnp.sum(grad_hidden, axis=0, keepdims=True)
        scaled = grad_hidden * gain_ref[...]
        grad_tok = inv_std * (
            scaled
            - jnp.mean(scaled, axis=-1, keepdims=True)
            - normed * jnp.mean(scaled * normed, axis=-1, keepdims=True)
        )
        grad_ref[k] = grad_tok.astype(BF16)

    @pl.when(step == pl.num_programs(1) - 1)
    def _():
        fold_s[...] = jnp.zeros_like(fold_s)
        for h in range(HEADS):
            for j in range(WLON):
                start = h * TL + (WLON - 1 - j) * COL
                fold_s[:, start : start + WT] += acc_s[
                    j * COL : (j + 1) * COL, h * WT : (h + 1) * WT
                ]
        for t in range(TW):
            dtable_ref[t, pl.ds(pl.multiple_of(band * COL, COL), COL), :] = fold_s[
                :, t * 128 : (t + 1) * 128
            ]

    @pl.when((band == pl.num_programs(0) - 1) & (step == pl.num_programs(1) - 1))
    def _():
        dense = jnp.concatenate([dwin_ref[...], dwout_ref[...]], axis=1)
        for t in range(4 * C // 128):
            dense_ref[t] = dense[:, t * 128 : (t + 1) * 128]
        small_ref[...] = jnp.zeros_like(small_ref)
        at = 0
        for ref in (dbin_ref, dbout_ref, dgain_ref, dshift_ref, dland_ref):
            width = ref.shape[1]
            for start in range(0, width, 128):
                size = min(128, width - start)
                small_ref[at : at + 1, :size] = ref[:, start : start + size]
                at += 1


def attend(tokens, cots, land, table, gate, gain, shift, w_in, b_in, w_out, land_gain, bands):
    count = tokens.shape[0]
    windows = count // bands
    per_step = 2 if windows % 2 == 0 else 1
    steps = windows // per_step

    def fixed(shape):
        return pl.BlockSpec(shape, lambda a, w: (0,) * len(shape))

    def per_band(shape):
        return pl.BlockSpec(shape, lambda a, w: (a,) + (0,) * (len(shape) - 1))

    win_spec = pl.BlockSpec((per_step, WT, C), lambda a, w: (a * steps + w, 0, 0))
    shapes = [(C, 3 * C), (1, 3 * C), (C, C), (1, C), (1, C), (1, C), (1, HL)]
    tiles = [(4 * C // 128, C, 128), (SMALL, 128), (TW, bands * COL, 128)]

    def body(*refs):
        kernel(windows, per_step, *refs)

    return pl.pallas_call(
        body,
        grid=(bands, steps),
        in_specs=[
            win_spec,
            win_spec,
            per_band((1, WT, windows)),
            per_band((1, DL, NPOS)),
            fixed((1, C)),
            fixed((1, C)),
            fixed((C, 3 * C)),
            fixed((3 * C, C)),
            fixed((1, 3 * C)),
            fixed((C, C)),
            fixed((1, HL)),
            per_band((1, COL, TL)),
        ],
        out_specs=[win_spec] + [fixed(t) for t in tiles],
        out_shape=[jax.ShapeDtypeStruct(tokens.shape, BF16)]
        + [jax.ShapeDtypeStruct(t, F32) for t in tiles],
        scratch_shapes=[pltpu.VMEM(t, F32) for t in shapes]
        + [pltpu.VMEM((WT, HL), F32), pltpu.VMEM((WT, HL), F32), pltpu.VMEM((COL, TW * 128), F32)],
        compiler_params=pltpu.CompilerParams(
            dimension_semantics=("arbitrary", "arbitrary"), vmem_limit_bytes=48 * 1024 * 1024
        ),
    )(
        tokens,
        cots,
        land,
        table,
        gain.reshape(1, C),
        shift.reshape(1, C),
        w_in,
        w_in.T,
        b_in.reshape(1, 3 * C),
        w_out.T,
        jnp.repeat(land_gain, WT).reshape(1, HL),
        gate,
    )


def ceil_to(n, m):
    return -(-n // m) * m


def exchange_kernel(
    n_lat,
    n_lon,
    t_chunk,
    d_chunk,
    dense_ref,
    small_ref,
    table_ref,
    dense_out,
    small_out,
    table_out,
    sq_out,
    s_lat,
    s_lon,
    d_own,
    t_own,
    d_lat,
    d_lon,
    t_lon,
    d_part,
    d_all,
    t_all,
    sq,
    lat_send,
    lat_recv,
    dl_send,
    dl_recv,
    tl_send,
    tl_recv,
    dg_send,
    dg_recv,
    tg_send,
    tg_recv,
    lg_send,
    lg_recv,
    sq_send,
    sq_recv,
    sl_send,
    sl_recv,
    so_send,
    so_recv,
):
    lat = lax.axis_index("lat")
    lon = lax.axis_index("lon")
    quarter = n_lon * d_chunk
    lat_peers = [(k, lax.rem(lat + k, n_lat)) for k in range(1, n_lat)]
    lon_peers = [(k, lax.rem(lon + k, n_lon)) for k in range(1, n_lon)]

    def rows(index, size):
        return pl.ds(pl.multiple_of(index * size, size), size)

    def send(src, dst, sends, recvs, k, target):
        copy = pltpu.make_async_remote_copy(
            src_ref=src,
            dst_ref=dst,
            send_sem=sends.at[k],
            recv_sem=recvs.at[k],
            device_id=target,
            device_id_type=pl.DeviceIdType.MESH,
        )
        copy.start()
        return copy

    barrier = pltpu.get_barrier_semaphore()
    for _, peer in lat_peers:
        pl.semaphore_signal(
            barrier, inc=1, device_id=(peer, lon), device_id_type=pl.DeviceIdType.MESH
        )
    for _, peer in lon_peers:
        pl.semaphore_signal(
            barrier, inc=1, device_id=(lat, peer), device_id_type=pl.DeviceIdType.MESH
        )
    d_rows = dense_ref.shape[0]
    t_rows = table_ref.shape[0]
    d_own[0:d_rows] = dense_ref[...].astype(BF16)
    if d_own.shape[0] > d_rows:
        d_own[d_rows:] = jnp.zeros((d_own.shape[0] - d_rows, 128), BF16)
    s_lat[lat] = small_ref[...]
    t_even = ceil_to(t_rows, 16)
    table = table_ref[...]
    if t_even > t_rows:
        table = jnp.concatenate([table, jnp.zeros((t_even - t_rows, 128), F32)], axis=0)
    t_own[0:t_even] = table.astype(BF16)
    if t_own.shape[0] > t_even:
        t_own[t_even:] = jnp.zeros((t_own.shape[0] - t_even, 128), BF16)
    pl.semaphore_wait(barrier, n_lat + n_lon - 2)

    s_copies = [
        send(s_lat.at[lat], s_lat.at[lat], sl_send, sl_recv, k - 1, (p, lon)) for k, p in lat_peers
    ]
    lat_copies = [
        send(d_own.at[rows(p, quarter)], d_lat.at[k - 1], lat_send, lat_recv, k - 1, (p, lon))
        for k, p in lat_peers
    ]
    t_copies = [
        send(t_own.at[rows(p, t_chunk)], t_lon.at[k - 1], tl_send, tl_recv, k - 1, (lat, p))
        for k, p in lon_peers
    ]
    for copy in s_copies:
        copy.wait()
    s_lon[lon] = functools.reduce(jnp.add, [s_lat[i] for i in range(n_lat)])
    so_copies = [
        send(s_lon.at[lon], s_lon.at[lon], so_send, so_recv, k - 1, (lat, p)) for k, p in lon_peers
    ]
    for copy in lat_copies:
        copy.wait()
    total = d_own[rows(lat, quarter)].astype(F32)
    for k, _ in lat_peers:
        total = total + d_lat[k - 1].astype(F32)
    d_part[...] = total.astype(BF16)
    d_copies = [
        send(d_part.at[rows(p, d_chunk)], d_lon.at[k - 1], dl_send, dl_recv, k - 1, (lat, p))
        for k, p in lon_peers
    ]
    for copy in t_copies:
        copy.wait()
    total = t_own[rows(lon, t_chunk)].astype(F32)
    for k, _ in lon_peers:
        total = total + t_lon[k - 1].astype(F32)
    t_mine = rows(lon, t_chunk)
    t_all[t_mine] = total.astype(BF16)
    tg_copies = [
        send(t_all.at[t_mine], t_all.at[t_mine], tg_send, tg_recv, k - 1, (lat, p))
        for k, p in lon_peers
    ]
    for copy in d_copies:
        copy.wait()
    total = d_part[rows(lon, d_chunk)].astype(F32)
    for k, _ in lon_peers:
        total = total + d_lon[k - 1].astype(F32)
    d_mine = rows(lat * n_lon + lon, d_chunk)
    d_all[d_mine] = total.astype(BF16)
    dg_copies = [
        send(d_all.at[d_mine], d_all.at[d_mine], dg_send, dg_recv, k - 1, (lat, p))
        for k, p in lon_peers
    ]
    for copy in tg_copies:
        copy.wait()
    summed = t_all[...].astype(F32)
    sq[0] = jnp.sum((summed * summed).reshape(summed.shape[0] // 8, 8, 128), axis=0)
    sq_copies = [
        send(sq.at[0], sq.at[k], sq_send, sq_recv, k - 1, (p, lon)) for k, p in lat_peers
    ]
    for copy in dg_copies:
        copy.wait()
    mine = rows(lat, quarter)
    lg_copies = [
        send(d_all.at[mine], d_all.at[mine], lg_send, lg_recv, k - 1, (p, lon))
        for k, p in lat_peers
    ]
    table_out[...] = summed
    for copy in sq_copies:
        copy.wait()
    squares = sq[0]
    for k, _ in lat_peers:
        squares = squares + sq[k]
    sq_out[...] = squares
    for copy in so_copies:
        copy.wait()
    small_out[...] = functools.reduce(jnp.add, [s_lon[i] for i in range(n_lon)])
    for copy in lg_copies:
        copy.wait()
    dense_out[...] = d_all[...].astype(F32)


def exchange(sizes, dense, small, table):
    n_lat, n_lon = sizes["lat"], sizes["lon"]
    t_chunk = ceil_to(-(-table.shape[0] // n_lon), 16)
    d_chunk = ceil_to(-(-dense.shape[0] // (n_lat * n_lon)), 16)
    t_total = n_lon * t_chunk
    d_total = n_lat * n_lon * d_chunk
    vmem = pl.BlockSpec(memory_space=pltpu.VMEM)

    def body(*refs):
        exchange_kernel(n_lat, n_lon, t_chunk, d_chunk, *refs)

    def sems(n):
        return [pltpu.SemaphoreType.DMA((n - 1,))] * 2

    return pl.pallas_call(
        body,
        in_specs=[vmem] * 3,
        out_specs=[vmem] * 4,
        out_shape=[
            jax.ShapeDtypeStruct((d_total, 128), F32),
            jax.ShapeDtypeStruct((SMALL, 128), F32),
            jax.ShapeDtypeStruct((t_total, 128), F32),
            jax.ShapeDtypeStruct((8, 128), F32),
        ],
        scratch_shapes=[
            pltpu.VMEM((n_lat, SMALL, 128), F32),
            pltpu.VMEM((n_lon, SMALL, 128), F32),
            pltpu.VMEM((d_total, 128), BF16),
            pltpu.VMEM((t_total, 128), BF16),
            pltpu.VMEM((n_lat - 1, n_lon * d_chunk, 128), BF16),
            pltpu.VMEM((n_lon - 1, d_chunk, 128), BF16),
            pltpu.VMEM((n_lon - 1, t_chunk, 128), BF16),
            pltpu.VMEM((n_lon * d_chunk, 128), BF16),
            pltpu.VMEM((d_total, 128), BF16),
            pltpu.VMEM((t_total, 128), BF16),
            pltpu.VMEM((n_lat, 8, 128), F32),
        ]
        + sems(n_lat)
        + sems(n_lon) * 4
        + sems(n_lat) * 3
        + sems(n_lon),
        compiler_params=pltpu.CompilerParams(
            collective_id=0, has_side_effects=True, vmem_limit_bytes=48 * 1024 * 1024
        ),
    )(dense, small, table)


def collapse_kernel(bands, count, table_ref, sq_ref, out_ref, fold_s):
    keep, pick = table_masks()
    total = jnp.sum(jnp.sum(sq_ref[...], axis=0, keepdims=True), axis=1, keepdims=True)
    factor = TARGET_RMS / jnp.sqrt(total / count + RMS_EPSILON)
    for band in range(bands):
        for t in range(TW):
            start = t * bands * COL + band * COL
            fold_s[:, t * 128 : (t + 1) * 128] = table_ref[start : start + COL]
        for h in range(HEADS):
            part = lax.dot_general(
                fold_s[:, h * TL : (h + 1) * TL].T * factor,
                pick,
                (((1,), (0,)), ((), ())),
                precision=lax.Precision.HIGHEST,
                preferred_element_type=F32,
            )
            part = part.reshape(DL, COL, HB) * keep[None]
            out_ref[band, :, h * HB : (h + 1) * HB] = jnp.sum(part, axis=1)


def collapse(bands, count, table, squares):
    vmem = pl.BlockSpec(memory_space=pltpu.VMEM)

    def body(*refs):
        collapse_kernel(bands, count, *refs)

    return pl.pallas_call(
        body,
        in_specs=[vmem] * 2,
        out_specs=vmem,
        out_shape=jax.ShapeDtypeStruct((bands, DL, NPOS), F32),
        scratch_shapes=[pltpu.VMEM((COL, TW * 128), F32)],
        compiler_params=pltpu.CompilerParams(vmem_limit_bytes=48 * 1024 * 1024),
    )(table, squares)


def normalize_rms(gradient):
    rms_value = jnp.sqrt(jnp.mean(gradient * gradient) + RMS_EPSILON)
    return gradient * (TARGET_RMS / rms_value)


def local(
    sizes,
    states,
    cotangent,
    land_mask,
    pole_mask,
    bias_table,
    norm_gain,
    norm_shift,
    in_weight,
    in_bias,
    out_weight,
    land_gain,
):
    rows = states.shape[1]
    cols = states.shape[2]
    bands = rows // WLAT
    windows = cols // WLON
    both = ("lat", "lon")
    lon_piece = jnp.stack([states[:, :, :S_LON], cotangent[:, :, :S_LON]])
    lat_piece = jnp.stack([states[:, :S_LAT, S_LON:], cotangent[:, :S_LAT, S_LON:]])
    land_low = land_mask.astype(BF16)
    pole_low = pole_mask.astype(BF16)
    lon_rim = moved(lon_piece, "lon", sizes, -1)
    lat_rim = moved(lat_piece, "lat", sizes, -1)
    corner = moved(lon_piece[:, :, :S_LAT], both, sizes, -1)
    land_ahead = jnp.concatenate([land_low[:, S_LON:], moved(land_low[:, :S_LON], "lon", sizes, -1)], axis=1)
    small = jnp.concatenate([land_ahead[:S_LAT], pole_low[:S_LAT, None]], axis=1)
    small_rim = moved(small, "lat", sizes, -1)
    rolled_land = jnp.concatenate([land_ahead[S_LAT:], small_rim[:, :cols]], axis=0).astype(F32)
    rolled_pole = jnp.concatenate([pole_low[S_LAT:], small_rim[:, cols]], axis=0).astype(F32)

    def windowed(own, at):
        top = jnp.concatenate([own[:, S_LAT:, S_LON:], lon_rim[at][:, S_LAT:]], axis=2)
        low = jnp.concatenate([lat_rim[at], corner[at]], axis=2)
        grid = jnp.concatenate([top, low], axis=1)
        return (
            grid.reshape(PL, bands, WLAT, cols, C)
            .transpose(1, 3, 0, 2, 4)
            .reshape(bands * windows, WT, C)
        )

    land_win = rolled_land.reshape(bands, WLAT, windows, WLON).transpose(0, 3, 1, 2)
    land_win = jnp.broadcast_to(
        land_win[:, :, None], (bands, WLON, PL, WLAT, windows)
    ).reshape(bands, WT, windows)
    total_rows = rows * sizes["lat"]
    row_ids = lax.axis_index("lat") * rows + jnp.arange(rows, dtype=jnp.int32)
    part = (row_ids >= total_rows - S_LAT).reshape(bands, WLAT)
    valid = (rolled_pole > 0.5).reshape(bands, WLAT)
    allowed = (part[:, :, None] == part[:, None, :]) & valid[:, :, None]
    gate = jnp.where(allowed[:, None, :, None, None, :], 0.0, FAR)
    gate = jnp.broadcast_to(gate, (bands, PL, WLAT, DL, PL, WLAT)).reshape(bands, COL, TL)
    outs = attend(
        windowed(states, 0),
        windowed(cotangent, 1),
        land_win,
        bias_table,
        gate,
        norm_gain,
        norm_shift,
        in_weight,
        in_bias,
        out_weight,
        land_gain,
        bands,
    )
    grad_win, dense, small, dtable = outs
    grad = (
        grad_win.reshape(bands, cols, PL, WLAT, C).transpose(2, 0, 3, 1, 4).reshape(PL, rows, cols, C)
    )
    below = moved(grad[:, rows - S_LAT :, : cols - S_LON], "lat", sizes, 1)
    behind = moved(grad[:, : rows - S_LAT, cols - S_LON :], "lon", sizes, 1)
    back_corner = moved(grad[:, rows - S_LAT :, cols - S_LON :], both, sizes, 1)
    upper = jnp.concatenate([back_corner, below], axis=2)
    lower = jnp.concatenate([behind, grad[:, : rows - S_LAT, : cols - S_LON]], axis=2)
    back = jnp.concatenate([upper, lower], axis=1)
    grad_states = (cotangent.astype(F32) + back.astype(F32)).astype(BF16)
    dense_sum, small_sum, table_sum, table_sq = exchange(
        sizes, dense.reshape(-1, 128), small, dtable.reshape(-1, 128)
    )
    table_count = bands * sizes["lat"] * DL * NPOS
    table_out = collapse(bands, table_count, table_sum, table_sq)
    dense_rows = 4 * C // 128 * C
    both_weights = (
        dense_sum[:dense_rows].reshape(4 * C // 128, C, 128).transpose(1, 0, 2).reshape(C, 4 * C)
    )
    vectors = []
    at = 0
    for width in (3 * C, C, C, C, HL):
        count = -(-width // 128)
        vectors.append(small_sum[at : at + count].reshape(-1)[:width])
        at += count
    dland = jnp.sum(vectors[4].reshape(HEADS, WT), axis=1)
    return (
        grad_states,
        normalize_rms(both_weights[:, : 3 * C]),
        normalize_rms(vectors[0]),
        normalize_rms(both_weights[:, 3 * C :]),
        normalize_rms(vectors[1]),
        normalize_rms(vectors[2]),
        normalize_rms(vectors[3]),
        normalize_rms(dland),
        table_out,
    )


def solution(mesh):
    sizes = dict(mesh.shape)

    def run(*args):
        return local(sizes, *args)

    return jax.shard_map(
        run,
        mesh=mesh,
        in_specs=(
            P(None, "lat", "lon", None),
            P(None, "lat", "lon", None),
            P("lat", "lon"),
            P("lat"),
            P("lat", None, None),
            P(),
            P(),
            P(),
            P(),
            P(),
            P(),
        ),
        out_specs=(
            P(None, "lat", "lon", None),
            P(),
            P(),
            P(),
            P(),
            P(),
            P(),
            P(),
            P("lat", None, None),
        ),
        check_vma=False,
    )
```

```python
import functools

import jax
import jax.numpy as jnp
from jax import lax
from jax.experimental import pallas as pl
from jax.experimental.pallas import tpu as pltpu
from jax.sharding import PartitionSpec as P

C = 192
HEADS = 6
HD = C // HEADS
PL = 2
WLAT = 12
WLON = 6
S_LAT = 6
S_LON = 3
WT = 144
DL = 11
NPOS = 3456
COL = PL * WLAT
HL = HEADS * WT
TL = DL * COL
TW = -(-HEADS * TL // 128)
HB = NPOS // HEADS
SMALL = 24

EPSILON = 1e-05
TARGET_RMS = 0.5
RMS_EPSILON = 1e-06
FAR = -1e30
F32 = jnp.float32
BF16 = jnp.bfloat16


def moved(array, axes, sizes, by):
    if isinstance(axes, str):
        size = sizes[axes]
        return lax.ppermute(array, axes, [(i, (i + by) % size) for i in range(size)])
    lat, lon = sizes["lat"], sizes["lon"]
    pairs = [
        (a * lon + b, ((a + by) % lat) * lon + (b + by) % lon)
        for a in range(lat)
        for b in range(lon)
    ]
    return lax.ppermute(array, axes, pairs)


def dot(a, b):
    return jnp.dot(a, b, preferred_element_type=F32)


def dot_nt(a, b):
    return lax.dot_general(a, b, (((1,), (1,)), ((), ())), preferred_element_type=F32)


def by_head(rows, head_masks):
    return jnp.concatenate([rows * m for m in head_masks], axis=0)


def diagonal(full):
    return jnp.concatenate(
        [full[HD * h : HD * (h + 1), WT * h : WT * (h + 1)] for h in range(HEADS)], axis=0
    )


def table_masks():
    row = lax.broadcasted_iota(jnp.int32, (COL, HB), 0)
    place = lax.broadcasted_iota(jnp.int32, (COL, HB), 1)
    q_level = place // (HB // 2)
    k_level = place // WT % 2
    q_row = place // WLAT % WLAT
    k_row = place % WLAT
    keep = (row == q_level * WLAT + q_row).astype(F32)
    pick = (row == k_level * WLAT + k_row).astype(F32).astype(BF16)
    return keep, pick


def kernel(
    windows,
    per_step,
    tok_ref,
    cot_ref,
    land_ref,
    table_ref,
    gain_ref,
    shift_ref,
    win_ref,
    win_t_ref,
    bin_ref,
    wout_t_ref,
    lg_ref,
    gate_ref,
    grad_ref,
    dense_ref,
    small_ref,
    dtable_ref,
    dwin_ref,
    dbin_ref,
    dwout_ref,
    dbout_ref,
    dgain_ref,
    dshift_ref,
    dland_ref,
    bias_s,
    acc_s,
    fold_s,
):
    band = pl.program_id(0)
    step = pl.program_id(1)
    scale = HD ** (-0.5)

    @pl.when((band == 0) & (step == 0))
    def _():
        for ref in (dwin_ref, dbin_ref, dwout_ref, dbout_ref, dgain_ref, dshift_ref, dland_ref):
            ref[...] = jnp.zeros_like(ref)

    @pl.when(step == 0)
    def _():
        acc_s[...] = jnp.zeros_like(acc_s)
        keep, pick = table_masks()
        for h in range(HEADS):
            own = table_ref[0, :, h * HB : (h + 1) * HB]
            spread = gate_ref[0]
            for _ in range(3):
                part = own.astype(BF16).astype(F32)
                own = own - part
                placed = (part[:, None, :] * keep[None]).reshape(TL, HB).astype(BF16)
                spread = spread + dot_nt(pick, placed)
            fold_s[:, h * TL : (h + 1) * TL] = spread
        for h in range(HEADS):
            for j in range(WLON):
                start = h * TL + (WLON - 1 - j) * COL
                bias_s[j * COL : (j + 1) * COL, h * WT : (h + 1) * WT] = fold_s[
                    :, start : start + WT
                ]

    lane = lax.broadcasted_iota(jnp.int32, (1, C), 1) // HD
    head_masks = [(lane == h).astype(F32).astype(BF16) for h in range(HEADS)]
    land_lane = lax.broadcasted_iota(jnp.int32, (1, windows), 1)

    for k in range(per_step):
        tok = tok_ref[k].astype(F32)
        center = tok - jnp.mean(tok, axis=-1, keepdims=True)
        inv_std = lax.rsqrt(jnp.mean(center * center, axis=-1, keepdims=True) + EPSILON)
        normed = center * inv_std
        hidden_f = normed * gain_ref[...] + shift_ref[...]
        hidden = hidden_f.astype(BF16)
        packed = (dot(hidden, win_ref[...]) + bin_ref[...]).astype(BF16)
        queries = packed[:, :C]
        keys = packed[:, C : 2 * C]
        values = packed[:, 2 * C :]
        q_heads = by_head(queries, head_masks)
        land = jnp.sum(
            jnp.where(land_lane == step * per_step + k, land_ref[0], 0.0), axis=1, keepdims=True
        )
        scores = dot_nt(keys, q_heads) * scale + bias_s[...] + land * lg_ref[...]
        top = jnp.max(scores, axis=0, keepdims=True)
        expd = jnp.exp(scores - top)
        probs = expd * (1.0 / jnp.sum(expd, axis=0, keepdims=True))
        probs_low = probs.astype(BF16)
        mixed_t = diagonal(dot(values.astype(F32).T.astype(BF16), probs_low)).astype(BF16)
        cot = cot_ref[k]
        dwout_ref[...] += dot(mixed_t, cot)
        dbout_ref[...] += jnp.sum(cot.astype(F32), axis=0, keepdims=True)
        grad_mixed = dot(cot, wout_t_ref[...]).astype(BF16)
        m_heads = by_head(grad_mixed, head_masks)
        grad_probs = dot_nt(values, m_heads)
        grad_values = dot(probs_low, m_heads)
        inner = jnp.sum(grad_probs * probs, axis=0, keepdims=True)
        grad_scores = probs * (grad_probs - inner)
        acc_s[...] += grad_scores
        dland_ref[...] += jnp.sum(grad_scores * land, axis=0, keepdims=True)
        scores_low = grad_scores.astype(BF16)
        grad_q = diagonal(dot(keys.astype(F32).T.astype(BF16), scores_low)).T * scale
        grad_k = dot(scores_low, q_heads) * scale
        grad_packed = jnp.concatenate([grad_q, grad_k, grad_values], axis=1)
        dbin_ref[...] += jnp.sum(grad_packed, axis=0, keepdims=True)
        packed_low = grad_packed.astype(BF16)
        dwin_ref[...] += dot(hidden_f.T.astype(BF16), packed_low)
        grad_hidden = dot(packed_low, win_t_ref[...])
        dgain_ref[...] += jnp.sum(grad_hidden * normed, axis=0, keepdims=True)
        dshift_ref[...] += jnp.sum(grad_hidden, axis=0, keepdims=True)
        scaled = grad_hidden * gain_ref[...]
        grad_tok = inv_std * (
            scaled
            - jnp.mean(scaled, axis=-1, keepdims=True)
            - normed * jnp.mean(scaled * normed, axis=-1, keepdims=True)
        )
        grad_ref[k] = grad_tok.astype(BF16)

    @pl.when(step == pl.num_programs(1) - 1)
    def _():
        fold_s[...] = jnp.zeros_like(fold_s)
        for h in range(HEADS):
            for j in range(WLON):
                start = h * TL + (WLON - 1 - j) * COL
                fold_s[:, start : start + WT] += acc_s[
                    j * COL : (j + 1) * COL, h * WT : (h + 1) * WT
                ]
        for t in range(TW):
            dtable_ref[t, pl.ds(pl.multiple_of(band * COL, COL), COL), :] = fold_s[
                :, t * 128 : (t + 1) * 128
            ]

    @pl.when((band == pl.num_programs(0) - 1) & (step == pl.num_programs(1) - 1))
    def _():
        dense = jnp.concatenate([dwin_ref[...], dwout_ref[...]], axis=1)
        for t in range(4 * C // 128):
            dense_ref[t] = dense[:, t * 128 : (t + 1) * 128]
        small_ref[...] = jnp.zeros_like(small_ref)
        at = 0
        for ref in (dbin_ref, dbout_ref, dgain_ref, dshift_ref, dland_ref):
            width = ref.shape[1]
            for start in range(0, width, 128):
                size = min(128, width - start)
                small_ref[at : at + 1, :size] = ref[:, start : start + size]
                at += 1


def attend(tokens, cots, land, table, gate, gain, shift, w_in, b_in, w_out, land_gain, bands):
    count = tokens.shape[0]
    windows = count // bands
    per_step = 2 if windows % 2 == 0 else 1
    steps = windows // per_step

    def fixed(shape):
        return pl.BlockSpec(shape, lambda a, w: (0,) * len(shape))

    def per_band(shape):
        return pl.BlockSpec(shape, lambda a, w: (a,) + (0,) * (len(shape) - 1))

    win_spec = pl.BlockSpec((per_step, WT, C), lambda a, w: (a * steps + w, 0, 0))
    shapes = [(C, 3 * C), (1, 3 * C), (C, C), (1, C), (1, C), (1, C), (1, HL)]
    tiles = [(4 * C // 128, C, 128), (SMALL, 128), (TW, bands * COL, 128)]

    def body(*refs):
        kernel(windows, per_step, *refs)

    return pl.pallas_call(
        body,
        grid=(bands, steps),
        in_specs=[
            win_spec,
            win_spec,
            per_band((1, WT, windows)),
            per_band((1, DL, NPOS)),
            fixed((1, C)),
            fixed((1, C)),
            fixed((C, 3 * C)),
            fixed((3 * C, C)),
            fixed((1, 3 * C)),
            fixed((C, C)),
            fixed((1, HL)),
            per_band((1, COL, TL)),
        ],
        out_specs=[win_spec] + [fixed(t) for t in tiles],
        out_shape=[jax.ShapeDtypeStruct(tokens.shape, BF16)]
        + [jax.ShapeDtypeStruct(t, F32) for t in tiles],
        scratch_shapes=[pltpu.VMEM(t, F32) for t in shapes]
        + [pltpu.VMEM((WT, HL), F32), pltpu.VMEM((WT, HL), F32), pltpu.VMEM((COL, TW * 128), F32)],
        compiler_params=pltpu.CompilerParams(
            dimension_semantics=("arbitrary", "arbitrary"), vmem_limit_bytes=48 * 1024 * 1024
        ),
    )(
        tokens,
        cots,
        land,
        table,
        gain.reshape(1, C),
        shift.reshape(1, C),
        w_in,
        w_in.T,
        b_in.reshape(1, 3 * C),
        w_out.T,
        jnp.repeat(land_gain, WT).reshape(1, HL),
        gate,
    )


def ceil_to(n, m):
    return -(-n // m) * m


def exchange_kernel(
    n_lat,
    n_lon,
    t_chunk,
    d_chunk,
    dense_ref,
    small_ref,
    table_ref,
    dense_out,
    small_out,
    table_out,
    sq_out,
    s_lat,
    s_lon,
    d_own,
    t_own,
    d_lat,
    d_lon,
    t_lon,
    d_part,
    d_all,
    t_all,
    sq,
    lat_send,
    lat_recv,
    dl_send,
    dl_recv,
    tl_send,
    tl_recv,
    dg_send,
    dg_recv,
    tg_send,
    tg_recv,
    lg_send,
    lg_recv,
    sq_send,
    sq_recv,
    sl_send,
    sl_recv,
    so_send,
    so_recv,
):
    lat = lax.axis_index("lat")
    lon = lax.axis_index("lon")
    quarter = n_lon * d_chunk
    lat_peers = [(k, lax.rem(lat + k, n_lat)) for k in range(1, n_lat)]
    lon_peers = [(k, lax.rem(lon + k, n_lon)) for k in range(1, n_lon)]

    def rows(index, size):
        return pl.ds(pl.multiple_of(index * size, size), size)

    def send(src, dst, sends, recvs, k, target):
        copy = pltpu.make_async_remote_copy(
            src_ref=src,
            dst_ref=dst,
            send_sem=sends.at[k],
            recv_sem=recvs.at[k],
            device_id=target,
            device_id_type=pl.DeviceIdType.MESH,
        )
        copy.start()
        return copy

    barrier = pltpu.get_barrier_semaphore()
    for _, peer in lat_peers:
        pl.semaphore_signal(
            barrier, inc=1, device_id=(peer, lon), device_id_type=pl.DeviceIdType.MESH
        )
    for _, peer in lon_peers:
        pl.semaphore_signal(
            barrier, inc=1, device_id=(lat, peer), device_id_type=pl.DeviceIdType.MESH
        )
    d_rows = dense_ref.shape[0]
    t_rows = table_ref.shape[0]
    d_own[0:d_rows] = dense_ref[...].astype(BF16)
    if d_own.shape[0] > d_rows:
        d_own[d_rows:] = jnp.zeros((d_own.shape[0] - d_rows, 128), BF16)
    s_lat[lat] = small_ref[...]
    t_even = ceil_to(t_rows, 16)
    table = table_ref[...]
    if t_even > t_rows:
        table = jnp.concatenate([table, jnp.zeros((t_even - t_rows, 128), F32)], axis=0)
    t_own[0:t_even] = table.astype(BF16)
    if t_own.shape[0] > t_even:
        t_own[t_even:] = jnp.zeros((t_own.shape[0] - t_even, 128), BF16)
    pl.semaphore_wait(barrier, n_lat + n_lon - 2)

    s_copies = [
        send(s_lat.at[lat], s_lat.at[lat], sl_send, sl_recv, k - 1, (p, lon)) for k, p in lat_peers
    ]
    lat_copies = [
        send(d_own.at[rows(p, quarter)], d_lat.at[k - 1], lat_send, lat_recv, k - 1, (p, lon))
        for k, p in lat_peers
    ]
    t_copies = [
        send(t_own.at[rows(p, t_chunk)], t_lon.at[k - 1], tl_send, tl_recv, k - 1, (lat, p))
        for k, p in lon_peers
    ]
    for copy in s_copies:
        copy.wait()
    s_lon[lon] = functools.reduce(jnp.add, [s_lat[i] for i in range(n_lat)])
    so_copies = [
        send(s_lon.at[lon], s_lon.at[lon], so_send, so_recv, k - 1, (lat, p)) for k, p in lon_peers
    ]
    for copy in lat_copies:
        copy.wait()
    total = d_own[rows(lat, quarter)].astype(F32)
    for k, _ in lat_peers:
        total = total + d_lat[k - 1].astype(F32)
    d_part[...] = total.astype(BF16)
    d_copies = [
        send(d_part.at[rows(p, d_chunk)], d_lon.at[k - 1], dl_send, dl_recv, k - 1, (lat, p))
        for k, p in lon_peers
    ]
    for copy in t_copies:
        copy.wait()
    total = t_own[rows(lon, t_chunk)].astype(F32)
    for k, _ in lon_peers:
        total = total + t_lon[k - 1].astype(F32)
    t_mine = rows(lon, t_chunk)
    t_all[t_mine] = total.astype(BF16)
    tg_copies = [
        send(t_all.at[t_mine], t_all.at[t_mine], tg_send, tg_recv, k - 1, (lat, p))
        for k, p in lon_peers
    ]
    for copy in d_copies:
        copy.wait()
    total = d_part[rows(lon, d_chunk)].astype(F32)
    for k, _ in lon_peers:
        total = total + d_lon[k - 1].astype(F32)
    d_mine = rows(lat * n_lon + lon, d_chunk)
    d_all[d_mine] = total.astype(BF16)
    dg_copies = [
        send(d_all.at[d_mine], d_all.at[d_mine], dg_send, dg_recv, k - 1, (lat, p))
        for k, p in lon_peers
    ]
    for copy in tg_copies:
        copy.wait()
    summed = t_all[...].astype(F32)
    sq[0] = jnp.sum((summed * summed).reshape(summed.shape[0] // 8, 8, 128), axis=0)
    sq_copies = [
        send(sq.at[0], sq.at[k], sq_send, sq_recv, k - 1, (p, lon)) for k, p in lat_peers
    ]
    for copy in dg_copies:
        copy.wait()
    mine = rows(lat, quarter)
    lg_copies = [
        send(d_all.at[mine], d_all.at[mine], lg_send, lg_recv, k - 1, (p, lon))
        for k, p in lat_peers
    ]
    table_out[...] = summed
    for copy in sq_copies:
        copy.wait()
    squares = sq[0]
    for k, _ in lat_peers:
        squares = squares + sq[k]
    sq_out[...] = squares
    for copy in so_copies:
        copy.wait()
    small_out[...] = functools.reduce(jnp.add, [s_lon[i] for i in range(n_lon)])
    for copy in lg_copies:
        copy.wait()
    dense_out[...] = d_all[...].astype(F32)


def exchange(sizes, dense, small, table):
    n_lat, n_lon = sizes["lat"], sizes["lon"]
    t_chunk = ceil_to(-(-table.shape[0] // n_lon), 16)
    d_chunk = ceil_to(-(-dense.shape[0] // (n_lat * n_lon)), 16)
    t_total = n_lon * t_chunk
    d_total = n_lat * n_lon * d_chunk
    vmem = pl.BlockSpec(memory_space=pltpu.VMEM)

    def body(*refs):
        exchange_kernel(n_lat, n_lon, t_chunk, d_chunk, *refs)

    def sems(n):
        return [pltpu.SemaphoreType.DMA((n - 1,))] * 2

    return pl.pallas_call(
        body,
        in_specs=[vmem] * 3,
        out_specs=[vmem] * 4,
        out_shape=[
            jax.ShapeDtypeStruct((d_total, 128), F32),
            jax.ShapeDtypeStruct((SMALL, 128), F32),
            jax.ShapeDtypeStruct((t_total, 128), F32),
            jax.ShapeDtypeStruct((8, 128), F32),
        ],
        scratch_shapes=[
            pltpu.VMEM((n_lat, SMALL, 128), F32),
            pltpu.VMEM((n_lon, SMALL, 128), F32),
            pltpu.VMEM((d_total, 128), BF16),
            pltpu.VMEM((t_total, 128), BF16),
            pltpu.VMEM((n_lat - 1, n_lon * d_chunk, 128), BF16),
            pltpu.VMEM((n_lon - 1, d_chunk, 128), BF16),
            pltpu.VMEM((n_lon - 1, t_chunk, 128), BF16),
            pltpu.VMEM((n_lon * d_chunk, 128), BF16),
            pltpu.VMEM((d_total, 128), BF16),
            pltpu.VMEM((t_total, 128), BF16),
            pltpu.VMEM((n_lat, 8, 128), F32),
        ]
        + sems(n_lat)
        + sems(n_lon) * 4
        + sems(n_lat) * 3
        + sems(n_lon),
        compiler_params=pltpu.CompilerParams(
            collective_id=0, has_side_effects=True, vmem_limit_bytes=48 * 1024 * 1024
        ),
    )(dense, small, table)


def collapse_kernel(bands, count, table_ref, sq_ref, out_ref, fold_s):
    keep, pick = table_masks()
    total = jnp.sum(jnp.sum(sq_ref[...], axis=0, keepdims=True), axis=1, keepdims=True)
    factor = TARGET_RMS / jnp.sqrt(total / count + RMS_EPSILON)
    for band in range(bands):
        for t in range(TW):
            start = t * bands * COL + band * COL
            fold_s[:, t * 128 : (t + 1) * 128] = table_ref[start : start + COL]
        for h in range(HEADS):
            part = dot(fold_s[:, h * TL : (h + 1) * TL].T.astype(BF16), pick)
            part = part.reshape(DL, COL, HB) * keep[None]
            out_ref[band, :, h * HB : (h + 1) * HB] = jnp.sum(part, axis=1) * factor


def collapse(bands, count, table, squares):
    vmem = pl.BlockSpec(memory_space=pltpu.VMEM)

    def body(*refs):
        collapse_kernel(bands, count, *refs)

    return pl.pallas_call(
        body,
        in_specs=[vmem] * 2,
        out_specs=vmem,
        out_shape=jax.ShapeDtypeStruct((bands, DL, NPOS), F32),
        scratch_shapes=[pltpu.VMEM((COL, TW * 128), F32)],
        compiler_params=pltpu.CompilerParams(vmem_limit_bytes=48 * 1024 * 1024),
    )(table, squares)


def normalize_rms(gradient):
    rms_value = jnp.sqrt(jnp.mean(gradient * gradient) + RMS_EPSILON)
    return gradient * (TARGET_RMS / rms_value)


def local(
    sizes,
    states,
    cotangent,
    land_mask,
    pole_mask,
    bias_table,
    norm_gain,
    norm_shift,
    in_weight,
    in_bias,
    out_weight,
    land_gain,
):
    rows = states.shape[1]
    cols = states.shape[2]
    bands = rows // WLAT
    windows = cols // WLON
    both = ("lat", "lon")
    lon_piece = jnp.stack([states[:, :, :S_LON], cotangent[:, :, :S_LON]])
    lat_piece = jnp.stack([states[:, :S_LAT, S_LON:], cotangent[:, :S_LAT, S_LON:]])
    land_low = land_mask.astype(BF16)
    lon_rim = moved(lon_piece, "lon", sizes, -1)
    lat_rim = moved(lat_piece, "lat", sizes, -1)
    corner = moved(lon_piece[:, :, :S_LAT], both, sizes, -1)
    land_lon = moved(land_low[:, :S_LON], "lon", sizes, -1)
    land_lat = moved(land_low[:S_LAT, S_LON:], "lat", sizes, -1)
    land_corner = moved(land_low[:S_LAT, :S_LON], both, sizes, -1)
    land_top = jnp.concatenate([land_low[S_LAT:, S_LON:], land_lon[S_LAT:]], axis=1)
    land_rest = jnp.concatenate([land_lat, land_corner], axis=1)
    rolled_land = jnp.concatenate([land_top, land_rest], axis=0).astype(F32)
    rolled_pole = jnp.concatenate([pole_mask[S_LAT:], jnp.ones((S_LAT,), jnp.int32)])

    def windowed(own, at):
        top = jnp.concatenate([own[:, S_LAT:, S_LON:], lon_rim[at][:, S_LAT:]], axis=2)
        low = jnp.concatenate([lat_rim[at], corner[at]], axis=2)
        grid = jnp.concatenate([top, low], axis=1)
        return (
            grid.reshape(PL, bands, WLAT, cols, C)
            .transpose(1, 3, 0, 2, 4)
            .reshape(bands * windows, WT, C)
        )

    land_win = rolled_land.reshape(bands, WLAT, windows, WLON).transpose(0, 3, 1, 2)
    land_win = jnp.broadcast_to(
        land_win[:, :, None], (bands, WLON, PL, WLAT, windows)
    ).reshape(bands, WT, windows)
    total_rows = rows * sizes["lat"]
    row_ids = lax.axis_index("lat") * rows + jnp.arange(rows, dtype=jnp.int32)
    part = (row_ids >= total_rows - S_LAT).reshape(bands, WLAT)
    valid = (rolled_pole > 0).reshape(bands, WLAT)
    allowed = (part[:, :, None] == part[:, None, :]) & valid[:, :, None]
    gate = jnp.where(allowed[:, None, :, None, None, :], 0.0, FAR)
    gate = jnp.broadcast_to(gate, (bands, PL, WLAT, DL, PL, WLAT)).reshape(bands, COL, TL)
    outs = attend(
        windowed(states, 0),
        windowed(cotangent, 1),
        land_win,
        bias_table,
        gate,
        norm_gain,
        norm_shift,
        in_weight,
        in_bias,
        out_weight,
        land_gain,
        bands,
    )
    grad_win, dense, small, dtable = outs
    grad = (
        grad_win.reshape(bands, cols, PL, WLAT, C).transpose(2, 0, 3, 1, 4).reshape(PL, rows, cols, C)
    )
    below = moved(grad[:, rows - S_LAT :, : cols - S_LON], "lat", sizes, 1)
    behind = moved(grad[:, : rows - S_LAT, cols - S_LON :], "lon", sizes, 1)
    back_corner = moved(grad[:, rows - S_LAT :, cols - S_LON :], both, sizes, 1)
    upper = jnp.concatenate([back_corner, below], axis=2)
    lower = jnp.concatenate([behind, grad[:, : rows - S_LAT, : cols - S_LON]], axis=2)
    back = jnp.concatenate([upper, lower], axis=1)
    grad_states = (cotangent.astype(F32) + back.astype(F32)).astype(BF16)
    dense_sum, small_sum, table_sum, table_sq = exchange(
        sizes, dense.reshape(-1, 128), small, dtable.reshape(-1, 128)
    )
    table_count = bands * sizes["lat"] * DL * NPOS
    table_out = collapse(bands, table_count, table_sum, table_sq)
    dense_rows = 4 * C // 128 * C
    both_weights = (
        dense_sum[:dense_rows].reshape(4 * C // 128, C, 128).transpose(1, 0, 2).reshape(C, 4 * C)
    )
    vectors = []
    at = 0
    for width in (3 * C, C, C, C, HL):
        count = -(-width // 128)
        vectors.append(small_sum[at : at + count].reshape(-1)[:width])
        at += count
    dland = jnp.sum(vectors[4].reshape(HEADS, WT), axis=1)
    return (
        grad_states,
        normalize_rms(both_weights[:, : 3 * C]),
        normalize_rms(vectors[0]),
        normalize_rms(both_weights[:, 3 * C :]),
        normalize_rms(vectors[1]),
        normalize_rms(vectors[2]),
        normalize_rms(vectors[3]),
        normalize_rms(dland),
        table_out,
    )


def solution(mesh):
    sizes = dict(mesh.shape)

    def run(*args):
        return local(sizes, *args)

    return jax.shard_map(
        run,
        mesh=mesh,
        in_specs=(
            P(None, "lat", "lon", None),
            P(None, "lat", "lon", None),
            P("lat", "lon"),
            P("lat"),
            P("lat", None, None),
            P(),
            P(),
            P(),
            P(),
            P(),
            P(),
        ),
        out_specs=(
            P(None, "lat", "lon", None),
            P(),
            P(),
            P(),
            P(),
            P(),
            P(),
            P(),
            P("lat", None, None),
        ),
        check_vma=False,
    )
```
